32 devices in a mesh: bx: 4 (over y, core), by: 8 (over z, x).
Axes of the slice: x: 2, y: 2, z: 4, core: 2. Of those that a mesh axis runs over, the one named last changes fastest.
Arguments:
- solution: float32 [4, 2048, 2048], P(None, 'by', 'bx'), may hold values from -6 to 6
- source: float32 [4, 2048, 2048], P(None, 'by', 'bx'), may hold values from -12 to 12
- class_ids: int32 [4, 2048, 2048], P(None, 'by', 'bx'), may hold values from 0 to 7
- conductivity: float32 [8], replicated, may hold values from 0.3 to 3
- spacing_x: float32 [2048], P('bx'), may hold values from 0.7 to 1.4
- spacing_y: float32 [2048], P('by'), may hold values from 0.7 to 1.4
- spacing_z: float32 [4], replicated, may hold values from 0.7 to 1.4
- forward_x: bfloat16 [2048, 2048], P('bx'), may hold values from -0.125 to 0.125
- forward_y: bfloat16 [2048, 2048], P('by'), may hold values from -0.125 to 0.125
- forward_z: bfloat16 [4, 4], replicated, may hold values from -3 to 3
- inverse_x: bfloat16 [2048, 2048], P('bx'), may hold values from -0.125 to 0.125
- inverse_y: bfloat16 [2048, 2048], P('by'), may hold values from -0.125 to 0.125
- inverse_z: bfloat16 [4, 4], replicated, may hold values from -3 to 3
- eigen_x: float32 [2048], P('bx'), may hold values from 0.05 to 4
- eigen_y: float32 [2048], P('by'), may hold values from 0.05 to 4
- eigen_z: float32 [4], replicated, may hold values from 0.05 to 4
Outputs:
- corrected: float32 [4, 2048, 2048], P(None, 'by', 'bx')
The draws below stay inside these ranges and needn't reach their ends.
All inputs are finite; a program needn't handle non-finite values.
Results may differ from the reference program's by a relative error of at most 0.0039.
Values may be sent and summed in bfloat16 or wider, within the bound.
No kernel may reach another device: no remote copies, remote signals or barrier semaphores. Data moves between devices by JAX's collectives and lax.ppermute only.
A program may use at most 64 MiB of HBM per device.

```python
import math
import jax
import jax.numpy as jnp
from jax import lax

NX = 2048
NY = 2048
Z = 4
CLASSES = 8


def touch_ends(entries, key, low, high):
    longest = entries.shape.index(max(entries.shape))
    spots = []
    for shift in (0, 1):
        where = [jax.random.randint(jax.random.fold_in(key, axis), (), 0, length) for axis, length in enumerate(entries.shape)]
        where[longest] = (where[longest] + shift) % entries.shape[longest]
        spots.append(tuple(where))
    return entries.at[spots[0]].set(low).at[spots[1]].set(high)


def level_of(rng, extent, cuts, low, largest):
    def one(dim, blocks):
        heights = jax.random.uniform(jax.random.fold_in(jax.random.fold_in(rng, 6), dim), (blocks,), jnp.float32, low / len(cuts), largest / len(cuts))
        return jnp.repeat(jnp.exp(heights), extent[dim] // blocks).reshape((-1,) + (1,) * (len(extent) - dim - 1))

    factor_of = one(*cuts[0])
    for cut in cuts[1:]:
        factor_of = factor_of * one(*cut)
    return factor_of


def normal_values(rng, extent, width, limit, pieces=(), held_as=jnp.bfloat16):
    values = width * jax.random.normal(rng, extent, jnp.float32)
    if pieces:
        values = values * level_of(rng, extent, pieces, -0.22, 0.18)
    return jnp.clip(values, -limit, limit).astype(held_as)


def setup_inputs(seed: int = 0) -> dict:
    key_of = jax.random.split(jax.random.key(seed), 17)
    solution = normal_values(key_of[0], (Z, NY, NX), 1.0, 6.0, ((1, 8), (2, 4)), jnp.float32)
    source = normal_values(key_of[1], (Z, NY, NX), 2.0, 12.0, ((1, 8), (2, 4)), jnp.float32)
    class_ids = touch_ends(jax.random.randint(key_of[2], (Z, NY, NX), 0, CLASSES), jax.random.fold_in(key_of[2], 1), 0, CLASSES - 1).astype(jnp.int32)
    conductivity = jnp.clip(jnp.exp(jax.random.uniform(key_of[3], (CLASSES,), jnp.float32, math.log(0.3), math.log(3.0))), 0.3, 3.0)
    spacing_x = jnp.clip(jnp.exp(math.log(1.4) - 0.6931472 * jax.random.uniform(key_of[4], (NX,), jnp.float32) ** level_of(key_of[4], (NX,), ((0, 4),), -0.2, 0.2)), 0.7, 1.4)
    spacing_y = jnp.clip(jnp.exp(math.log(1.4) - 0.6931472 * jax.random.uniform(key_of[5], (NY,), jnp.float32) ** level_of(key_of[5], (NY,), ((0, 8),), -0.2, 0.2)), 0.7, 1.4)
    spacing_z = jnp.clip(jnp.exp(jax.random.uniform(key_of[6], (Z,), jnp.float32, math.log(0.7), math.log(1.4))), 0.7, 1.4)
    forward_x = normal_values(key_of[7], (NX, NX), NX ** -0.5, 0.125, ((0, 4),))
    forward_y = normal_values(key_of[8], (NY, NY), NY ** -0.5, 0.125, ((0, 8),))
    forward_z = normal_values(key_of[9], (Z, Z), Z ** -0.5, 3.0)
    inverse_x = normal_values(key_of[10], (NX, NX), NX ** -0.5, 0.125, ((0, 4),))
    inverse_y = normal_values(key_of[11], (NY, NY), NY ** -0.5, 0.125, ((0, 8),))
    inverse_z = normal_values(key_of[12], (Z, Z), Z ** -0.5, 3.0)
    eigen_x = jnp.clip(jnp.exp(math.log(4.0) - 4.3820266 * jax.random.uniform(key_of[13], (NX,), jnp.float32) ** level_of(key_of[13], (NX,), ((0, 4),), -0.2, 0.2)), 0.05, 4.0)
    eigen_y = jnp.clip(jnp.exp(math.log(4.0) - 4.3820266 * jax.random.uniform(key_of[14], (NY,), jnp.float32) ** level_of(key_of[14], (NY,), ((0, 8),), -0.2, 0.2)), 0.05, 4.0)
    eigen_z = jnp.clip(jnp.exp(jax.random.uniform(key_of[15], (Z,), jnp.float32, math.log(0.05), math.log(4.0))), 0.05, 4.0)
    return dict(solution=solution, source=source, class_ids=class_ids, conductivity=conductivity, spacing_x=spacing_x, spacing_y=spacing_y, spacing_z=spacing_z, forward_x=forward_x, forward_y=forward_y, forward_z=forward_z, inverse_x=inverse_x, inverse_y=inverse_y, inverse_z=inverse_z, eigen_x=eigen_x, eigen_y=eigen_y, eigen_z=eigen_z)


shift_value = 0.1


def coefficients(class_ids, conductivity):
    result = jnp.zeros(class_ids.shape, jnp.float32)
    for index in range(CLASSES):
        result = result + jnp.where(class_ids == index, conductivity[index], jnp.float32(0.0))
    return result


def operate(field, coef):
    padded = jnp.pad(field, 1)
    padcoef = jnp.pad(coef, 1)
    center = padded[1:-1, 1:-1, 1:-1]
    ccoef = padcoef[1:-1, 1:-1, 1:-1]
    slices = [(slice(2, None), slice(1, -1), slice(1, -1)), (slice(0, -2), slice(1, -1), slice(1, -1)),
              (slice(1, -1), slice(2, None), slice(1, -1)), (slice(1, -1), slice(0, -2), slice(1, -1)),
              (slice(1, -1), slice(1, -1), slice(2, None)), (slice(1, -1), slice(1, -1), slice(0, -2))]
    result = jnp.zeros(field.shape, jnp.float32)
    for where_at in slices:
        neighbour = padded[where_at]
        ncoef = padcoef[where_at]
        face = jnp.where(ncoef > 0, 2.0 * ccoef * ncoef / (ccoef + ncoef), ccoef)
        result = result + face * (center - neighbour)
    return result


def reference(solution, source, class_ids, conductivity, spacing_x, spacing_y, spacing_z, forward_x, forward_y, forward_z, inverse_x, inverse_y, inverse_z, eigen_x, eigen_y, eigen_z):
    highest = lax.Precision.HIGHEST
    coef = coefficients(class_ids, conductivity)
    operated = operate(solution, coef)
    weights = spacing_z[:, None, None] * spacing_y[None, :, None] * spacing_x[None, None, :]
    restricted = (weights * (source - operated)).astype(jnp.bfloat16)
    half = jnp.einsum('kji,mi->kjm', restricted.astype(jnp.float32), forward_x.astype(jnp.float32), precision=highest)
    modes_xy = jnp.einsum('kjm,nj->knm', half, forward_y.astype(jnp.float32), precision=highest)
    modes = jnp.einsum('qk,knm->qnm', forward_z.astype(jnp.float32), modes_xy, precision=highest)
    divisor = eigen_x[None, None, :] + eigen_y[None, :, None] + eigen_z[:, None, None] + shift_value
    scaled = modes / divisor
    spectral = jnp.einsum('kq,qnm->knm', inverse_z.astype(jnp.float32), scaled, precision=highest).astype(jnp.bfloat16)
    partial_x = jnp.einsum('knm,im->kni', spectral.astype(jnp.float32), inverse_x.astype(jnp.float32), precision=highest)
    field = jnp.einsum('kni,jn->kji', partial_x, inverse_y.astype(jnp.float32), precision=highest)
    return solution + weights * field
```

```python
import functools

import jax
import jax.numpy as jnp
from jax import lax
from jax.experimental import pallas as pl
from jax.experimental.pallas import tpu as pltpu
from jax.sharding import PartitionSpec as P

CLASSES = 8
LANES = 128
SUBLANES = 8
ROWS = 16
MIB = 1 << 20

shift_value = 0.1

VMEM = pl.BlockSpec(memory_space=pltpu.VMEM)
SMEM = pl.BlockSpec(memory_space=pltpu.SMEM)
NT = (((1,), (1,)), ((), ()))


def reciprocal(value):
    guess = pl.reciprocal(value, approx=True)
    return guess * (2.0 - value * guess)


def column_of(row):
    return jnp.broadcast_to(row, (LANES, LANES)).T


def lookup(classes, table):
    value = jnp.full(classes.shape, table[0], jnp.float32)
    for index in range(1, CLASSES):
        value = jnp.where(classes == index, table[index], value)
    return value


def shift_outer(value, axis, step):
    size = lax.axis_size(axis)
    return lax.ppermute(value, axis, [(i, (i + 2 * step) % size) for i in range(size)])


def swap_inner(value, axis):
    size = lax.axis_size(axis)
    return lax.ppermute(value, axis, [(i, i ^ 1) for i in range(size)])


def after(value, *given):
    return lax.optimization_barrier((value, given))[0]


def neighbours(first, last, axis):
    size = lax.axis_size(axis)
    up = [(i, i + 1) for i in range(size - 1)]
    down = [(j, i) for i, j in up]
    return lax.ppermute(last, axis, up), lax.ppermute(first, axis, down)


def spread(value, axis):
    size = lax.axis_size(axis)
    pieces = {}
    for step in range(size // 2):
        kept = value if step == 0 else shift_outer(value, axis, step)
        pieces[step, 0] = kept
        pieces[step, 1] = swap_inner(kept, axis)
    return pieces


def owner(index, size, step, swapped):
    outer = size // 2
    place = lax.rem(index // 2 + (outer - step), outer)
    return 2 * place + (1 - lax.rem(index, 2) if swapped else lax.rem(index, 2))


def faces_kernel(half_ref, sol_ref, cls_ref, left_ref, right_ref, top_ref, bottom_ref):
    planes, rows, columns = sol_ref.shape
    table = [half_ref[i] for i in range(CLASSES)]
    lane = lax.broadcasted_iota(jnp.int32, (rows, LANES), 1)
    for ref, place, at in ((left_ref, 0, 0), (right_ref, columns - LANES, LANES - 1)):
        result = jnp.zeros((rows, LANES), jnp.float32)
        classes = jnp.zeros((rows, LANES), jnp.int32)
        for k in range(planes):
            shift = (k - at) % LANES
            value = sol_ref[k, :, place : place + LANES]
            held = cls_ref[k, :, place : place + LANES]
            if shift:
                value = pltpu.roll(value, shift, 1)
            result = jnp.where(lane == k, value, result)
            shift = (planes + k - at) % LANES
            if shift:
                held = pltpu.roll(held, shift, 1)
            classes = jnp.where(lane == planes + k, held, classes)
        ref[...] = jnp.where(lane < planes, result, lookup(classes, table))
    for ref, place in ((top_ref, 0), (bottom_ref, rows - 1)):
        ref[0] = sol_ref[:, place, :]
        ref[1] = lookup(cls_ref[:, place, :], table)


def cut_kernel(place_ref, matrix_ref, eigen_ref, out_ref):
    rows, width = matrix_ref.shape[0], out_ref.shape[1]
    at = pl.multiple_of(place_ref[2] * width, LANES)
    out_ref[:rows, :] = matrix_ref[:, pl.ds(at, width)]
    left = eigen_ref[...]
    row = lax.broadcasted_iota(jnp.int32, (ROWS, rows), 0)
    result = jnp.zeros((ROWS, rows), jnp.float32)
    for index in range(3):
        term = left.astype(jnp.bfloat16).astype(jnp.float32)
        result = jnp.where(row == index, term, result)
        left = left - term
    if width > rows:
        result = jnp.concatenate([result, jnp.zeros((ROWS, width - rows), jnp.float32)], axis=1)
    out_ref[rows:, :] = result.astype(jnp.bfloat16)


def others_kernel(zs, place_ref, blocks_ref, out_ref):
    for step in range(1, zs):
        out_ref[step - 1] = blocks_ref[lax.rem(place_ref[0] + (zs - step), zs)]


def stencil_kernel(
    low,
    half_ref,
    wz_ref,
    sol_ref,
    cls_ref,
    src_ref,
    left_ref,
    right_ref,
    top_ref,
    bottom_ref,
    wy_ref,
    wx_ref,
    out_ref,
    u_ref,
    h_ref,
    sides_ref,
    wy_col,
):
    planes, rows, columns = sol_ref.shape
    count = out_ref.shape[0]
    table = [half_ref[i] for i in range(CLASSES)]
    first, last = max(low - 1, 0), min(low + count, planes - 1)
    pad = SUBLANES
    for k in range(first, last + 1):
        slot = k - first
        u_ref[slot, pl.ds(pad, rows), :] = sol_ref[k]

        def fill(step, _, k=k, slot=slot):
            at = pl.multiple_of(step * 2 * SUBLANES, 2 * SUBLANES)
            h_ref[slot, pl.ds(pad + at, 2 * SUBLANES), :] = lookup(
                cls_ref[k, pl.ds(at, 2 * SUBLANES), :], table
            )
            return 0

        lax.fori_loop(0, rows // (2 * SUBLANES), fill, 0)
    for k in range(low, low + count):
        slot = k - first
        for ref, place, edge in ((top_ref, 0, pad), (bottom_ref, pad + rows, pad + rows - 1)):
            value, held = ref[0, k : k + 1, :], ref[1, k : k + 1, :]
            held = jnp.where(held > 0, held, h_ref[slot, edge : edge + 1, :])
            u_ref[slot, place : place + pad, :] = jnp.broadcast_to(value, (pad, columns))
            h_ref[slot, place : place + pad, :] = jnp.broadcast_to(held, (pad, columns))
        lane = lax.broadcasted_iota(jnp.int32, (rows, LANES), 1)
        for part in range(2):
            at = part * planes + k
            before = left_ref[...]
            after = right_ref[...]
            before = pltpu.roll(before, (LANES - at) % LANES, 1) if at else before
            after = pltpu.roll(after, (LANES - 1 - at) % LANES, 1)
            sides_ref[k - low, part] = jnp.where(lane < LANES // 2, before, after)
    for block in range(rows // LANES):
        wy_col[pl.ds(block * LANES, LANES), :] = column_of(
            wy_ref[:, block * LANES : (block + 1) * LANES]
        )
    wx = wx_ref[...]
    size = 2 * SUBLANES
    tiles = columns // LANES

    def block(step, _):
        at = pl.multiple_of(step * size, size)
        wide = size + 2 * pad
        lane = lax.broadcasted_iota(jnp.int32, (size, columns), 1)
        wy = jnp.tile(wy_col[pl.ds(at, size), :], (1, tiles)) * wx
        below = None
        if low > 0:
            below = (u_ref[0, pl.ds(pad + at, size), :], h_ref[0, pl.ds(pad + at, size), :])
        carried = None
        for k in range(low, low + count):
            slot = k - first
            uw = u_ref[slot, pl.ds(at, wide), :]
            hw = h_ref[slot, pl.ds(at, wide), :]
            u, h = uw[pad : pad + size], hw[pad : pad + size]
            total = (u - pltpu.roll(uw, 1, 0)[pad : pad + size]) * reciprocal(
                h + pltpu.roll(hw, 1, 0)[pad : pad + size]
            )
            total += (u - pltpu.roll(uw, wide - 1, 0)[pad : pad + size]) * reciprocal(
                h + pltpu.roll(hw, wide - 1, 0)[pad : pad + size]
            )
            su = sides_ref[k - low, 0, pl.ds(at, size), :]
            sh = sides_ref[k - low, 1, pl.ds(at, size), :]
            if tiles > 1:
                zeros = jnp.zeros((size, columns - LANES), jnp.float32)
                su_after = jnp.concatenate([zeros, su], axis=1)
                sh_after = jnp.concatenate([zeros, sh], axis=1)
            else:
                su_after, sh_after = su, sh
            sh_after = jnp.where(sh_after > 0, sh_after, h)
            final = lane == columns - 1
            un = jnp.where(final, su_after, pltpu.roll(u, columns - 1, 1))
            hn = jnp.where(final, sh_after, pltpu.roll(h, columns - 1, 1))
            flux = (u - un) * reciprocal(h + hn)
            u0, h0 = u[:, :LANES], h[:, :LANES]
            start = (su - u0) * reciprocal(h0 + jnp.where(sh > 0, sh, h0))
            if tiles > 1:
                zeros = jnp.zeros((size, columns - LANES), jnp.float32)
                start = jnp.concatenate([start, zeros], axis=1)
            total += flux - jnp.where(lane == 0, start, pltpu.roll(flux, 1, 1))
            if k == 0:
                total += u * reciprocal(h + h)
            elif carried is not None:
                total -= carried
            else:
                total += (u - below[0]) * reciprocal(h + below[1])
            if k == planes - 1:
                total += u * reciprocal(h + h)
            else:
                ua = u_ref[slot + 1, pl.ds(pad + at, size), :]
                ha = h_ref[slot + 1, pl.ds(pad + at, size), :]
                carried = (u - ua) * reciprocal(h + ha)
                total += carried
            result = (wz_ref[k] * wy) * (src_ref[k, pl.ds(at, size), :] - total)
            out_ref[k - low, pl.ds(at, size), :] = result.astype(jnp.bfloat16)
        return 0

    lax.fori_loop(0, rows // size, block, 0)


def forward_x_kernel(sizes, names, place_ref, matrix_ref, *refs):
    bx, zs = sizes
    pieces, outs, held = refs[: len(names)], refs[len(names) : -1], refs[-1]
    z, me = place_ref[0], place_ref[2]
    count, rows, columns = pieces[0].shape
    part = held.shape[1]
    for k in range(count):
        total = None
        for name, ref in zip(names, pieces):
            at = pl.multiple_of(owner(me, bx, *name) * columns, LANES)
            term = lax.dot_general(
                matrix_ref[:, pl.ds(at, columns)], ref[k], NT, preferred_element_type=jnp.float32
            )
            total = term if total is None else total + term
        for block in range(zs):
            held[block] = total[block * part : (block + 1) * part].astype(jnp.bfloat16)
        for step in range(zs):
            outs[step][k] = held[lax.rem(z + step, zs)]


def joined(line, first, count):
    return jnp.concatenate([line[first + i] for i in range(count)], axis=1)


def middle_kernel(
    sizes, names, chunks, place_ref, fz_ref, iz_ref, ez_ref, ex_ref, ey_ref, own_ref, *refs
):
    bx, zs = sizes
    shares, refs = refs[: len(names)], refs[len(names) :]
    pieces, refs = refs[: 2 * chunks], refs[2 * chunks :]
    outs, (line, modes, ex_col) = refs[:chunks], refs[chunks:]
    z, x, me = place_ref[0], place_ref[1], place_ref[2]
    count, part, _ = pieces[0].shape
    planes = count * chunks
    rows = own_ref.shape[0]
    quarter = shares[0].shape[2]
    for chunk in range(chunks):
        for swapped in range(2):
            for place in range(zs):
                block = 2 * place + (1 - x if swapped else x)
                for k in range(count):
                    line[block, (chunk * count + k) * part : (chunk * count + k + 1) * part, :] = (
                        pieces[2 * chunk + swapped][k, :, place * rows : (place + 1) * rows]
                    )
    at = pl.multiple_of(z * part, LANES)
    ex_col[...] = column_of(ex_ref[:, pl.ds(at, part)])
    tiles = rows // LANES
    for step in range(zs):
        if step == 0:
            total = lax.dot_general(
                joined(line, 0, 2 * zs), own_ref[...], NT, preferred_element_type=jnp.float32
            )
        else:
            total = None
            for name, ref in zip(names, shares):
                term = lax.dot_general(
                    joined(line, owner(me, bx, *name) * (quarter // rows), quarter // rows),
                    ref[step - 1, :rows],
                    NT,
                    preferred_element_type=jnp.float32,
                )
                total = term if total is None else total + term
        modes[...] = total
        ey = ey_ref[...]
        if step > 0:
            ey = jnp.sum(shares[0][step - 1, rows:, :rows].astype(jnp.float32), 0, keepdims=True)
        ey += shift_value

        def mix(at, _, step=step, ey=ey):
            at = pl.multiple_of(at * ROWS, ROWS)
            ex = jnp.tile(ex_col[pl.ds(at, ROWS), :], (1, tiles)) + ey
            given = [modes[pl.ds(k * part + at, ROWS), :] for k in range(planes)]
            scaled = []
            for q in range(planes):
                value = fz_ref[q, 0] * given[0]
                for k in range(1, planes):
                    value += fz_ref[q, k] * given[k]
                scaled.append(value * reciprocal(ex + ez_ref[q]))
            for k in range(planes):
                value = iz_ref[k, 0] * scaled[0]
                for q in range(1, planes):
                    value += iz_ref[k, q] * scaled[q]
                outs[k // count][k % count, pl.ds(at, ROWS), step * rows : (step + 1) * rows] = (
                    value.astype(jnp.bfloat16)
                )
            return 0

        lax.fori_loop(0, part // ROWS, mix, 0)


def inverse_y_kernel(sizes, names, place_ref, own_ref, *refs):
    bx, zs = sizes
    shares, refs = refs[: len(names)], refs[len(names) :]
    spectra, outs, line = refs[:2], refs[2:-1], refs[-1]
    z, x, me = place_ref[0], place_ref[1], place_ref[2]
    count, part, _ = spectra[0].shape
    rows = own_ref.shape[0]
    quarter = shares[0].shape[2]
    for swapped in range(2):
        for step in range(zs):
            block = 2 * lax.rem(z + (zs - step), zs) + (1 - x if swapped else x)
            for k in range(count):
                line[block, k * part : (k + 1) * part, :] = spectra[swapped][
                    k, :, step * rows : (step + 1) * rows
                ]
    for step in range(zs):
        if step == 0:
            total = lax.dot_general(
                own_ref[...], joined(line, 0, 2 * zs), NT, preferred_element_type=jnp.float32
            )
        else:
            total = None
            for name, ref in zip(names, shares):
                term = lax.dot_general(
                    ref[zs - step - 1, :rows],
                    joined(line, owner(me, bx, *name) * (quarter // rows), quarter // rows),
                    NT,
                    preferred_element_type=jnp.float32,
                )
                total = term if total is None else total + term
        for k in range(count):
            outs[step][k] = total[:, k * part : (k + 1) * part].astype(jnp.bfloat16)


def merge_kernel(zs, place_ref, *refs):
    pieces, out = refs[:-1], refs[-1]
    part = pieces[0].shape[2]
    for step, ref in enumerate(pieces):
        at = pl.multiple_of(lax.rem(place_ref[0] + (zs - step), zs) * part, LANES)
        out[:, :, pl.ds(at, part)] = ref[...]


def inverse_x_kernel(bx, names, low, place_ref, wz_ref, wy_ref, wx_ref, sol_ref, matrix_ref, *refs):
    pieces, out_ref, wy_col = refs[: len(names)], refs[-2], refs[-1]
    me = place_ref[2]
    k = pl.program_id(0)
    rows, columns = out_ref.shape[1:]
    width = pieces[0].shape[2]
    for block in range(rows // LANES):
        wy_col[pl.ds(block * LANES, LANES), :] = column_of(
            wy_ref[:, block * LANES : (block + 1) * LANES]
        )
    total = None
    for name, ref in zip(names, pieces):
        at = pl.multiple_of(owner(me, bx, *name) * width, LANES)
        term = lax.dot_general(
            ref[k], matrix_ref[:, pl.ds(at, width)], NT, preferred_element_type=jnp.float32
        )
        total = term if total is None else total + term
    weight = wz_ref[low + k] * (jnp.tile(wy_col[...], (1, columns // LANES)) * wx_ref[...])
    out_ref[0] = sol_ref[0] + weight * total


def params(mib):
    return pltpu.CompilerParams(vmem_limit_bytes=mib * MIB)


def cost(flops, nbytes):
    return pl.CostEstimate(flops=flops // 16, bytes_accessed=nbytes // 16, transcendentals=0)


def on_device_tiled(
    solution,
    source,
    class_ids,
    conductivity,
    spacing_x,
    spacing_y,
    spacing_z,
    forward_x,
    forward_y,
    forward_z,
    inverse_x,
    inverse_y,
    inverse_z,
    eigen_x,
    eigen_y,
    eigen_z,
):
    f32, bf16 = jnp.float32, jnp.bfloat16
    bx, by = lax.axis_size("bx"), lax.axis_size("by")
    zs = by // 2
    sizes = (bx, zs)
    planes, rows, columns = solution.shape
    part = columns // zs
    length = forward_y.shape[1]
    chunks = 2 if planes % 2 == 0 else 1
    count = planes // chunks
    at_x, at_y = lax.axis_index("bx"), lax.axis_index("by")
    place = jnp.stack([at_y // 2, at_y % 2, at_x]).astype(jnp.int32)
    half = 0.5 / conductivity
    fz, iz = forward_z.astype(f32), inverse_z.astype(f32)
    wx, wy = spacing_x.reshape(1, -1), spacing_y.reshape(1, -1)

    quarter = length // bx

    def cut(matrix, eigen):
        mine = pl.pallas_call(
            cut_kernel,
            out_shape=jax.ShapeDtypeStruct((rows + ROWS, quarter), bf16),
            in_specs=[SMEM, VMEM, VMEM],
            out_specs=VMEM,
            compiler_params=params(4),
            cost_estimate=cost(1 << 20, 1 << 20),
            name="cut",
        )(place, matrix, eigen)
        groups = [[2 * i + j for i in range(zs)] for j in range(2)]
        return lax.all_gather(mine, "by", axis_index_groups=groups)

    def others(gathered):
        return pl.pallas_call(
            functools.partial(others_kernel, zs),
            out_shape=jax.ShapeDtypeStruct((zs - 1, rows + ROWS, quarter), bf16),
            in_specs=[SMEM, VMEM],
            out_specs=VMEM,
            compiler_params=params(4),
            cost_estimate=cost(1 << 20, 1 << 20),
            name="others",
        )(place, gathered)

    def merge(pieces):
        count, rows, width = pieces[0].shape
        return pl.pallas_call(
            functools.partial(merge_kernel, zs),
            out_shape=jax.ShapeDtypeStruct((count, rows, zs * width), bf16),
            in_specs=[SMEM] + [VMEM] * zs,
            out_specs=VMEM,
            compiler_params=params(8),
            cost_estimate=cost(1 << 20, 1 << 20),
            name="merge",
        )(place, *pieces)

    def exchange(pieces):
        return merge(
            [
                piece if step == 0 else shift_outer(piece, "by", step)
                for step, piece in enumerate(pieces)
            ]
        )

    left, right, top, bottom = pl.pallas_call(
        faces_kernel,
        out_shape=(
            jax.ShapeDtypeStruct((rows, LANES), f32),
            jax.ShapeDtypeStruct((rows, LANES), f32),
            jax.ShapeDtypeStruct((2, planes, columns), f32),
            jax.ShapeDtypeStruct((2, planes, columns), f32),
        ),
        in_specs=[SMEM, VMEM, VMEM],
        out_specs=[VMEM] * 4,
        compiler_params=params(12),
        cost_estimate=cost(1 << 20, 1 << 20),
        name="faces",
    )(half, solution, class_ids)
    left, right = neighbours(left, right, "bx")
    top, bottom = neighbours(top, bottom, "by")

    ey = eigen_y.reshape(1, -1)
    names = tuple((step, swapped) for step in range(bx // 2) for swapped in range(2))

    gathered = []
    for chunk in range(chunks):
        low = chunk * count
        held = min(low + count, planes - 1) - max(low - 1, 0) + 1
        restricted = pl.pallas_call(
            functools.partial(stencil_kernel, low),
            out_shape=jax.ShapeDtypeStruct((count, rows, columns), bf16),
            in_specs=[SMEM, SMEM] + [VMEM] * 9,
            out_specs=VMEM,
            scratch_shapes=[
                pltpu.VMEM((held, rows + 2 * SUBLANES, columns), f32),
                pltpu.VMEM((held, rows + 2 * SUBLANES, columns), f32),
                pltpu.VMEM((count, 2, rows, LANES), f32),
                pltpu.VMEM((rows, LANES), f32),
            ],
            compiler_params=params(24),
            cost_estimate=cost(1 << 26, 8 << 20),
            name="stencil",
        )(half, spacing_z, solution, class_ids, source, left, right, top, bottom, wy, wx)
        gathered.append(restricted)
    highest = lax.Precision.HIGHEST
    restricted = jnp.concatenate(gathered, axis=0)
    weights = spacing_z[:, None, None] * spacing_y[None, :, None] * spacing_x[None, None, :]
    modes_xy = x_high(y_low(restricted, forward_y), forward_x)
    modes = jnp.einsum("qk,knm->qnm", fz, modes_xy, precision=highest)
    divisor = eigen_x[None, None, :] + eigen_y[None, :, None] + eigen_z[:, None, None] + shift_value
    spectral = jnp.einsum("kq,qnm->knm", iz, modes / divisor, precision=highest).astype(bf16)
    field = x_high(y_low(spectral, inverse_y), inverse_x)
    return solution + weights * field


def extended(value, sides, width):
    for axis, dim in sides:
        size, length = (lax.axis_size(axis), value.shape[dim])
        up = [(i, (i + 1) % size) for i in range(size - 1)]
        down = [(j, i) for i, j in up]
        last = lax.slice_in_dim(value, length - width, length, axis=dim)
        first = lax.slice_in_dim(value, 0, width, axis=dim)
        before = lax.ppermute(last, axis, up)
        after = lax.ppermute(first, axis, down)
        value = jnp.concatenate([before, value, after], axis=dim)
    return value


def coefficients(class_ids, conductivity):
    result = jnp.zeros(class_ids.shape, jnp.float32)
    for index in range(CLASSES):
        result = result + jnp.where(class_ids == index, conductivity[index], jnp.float32(0.0))
    return result


def operate(solution, coef):
    stacked = jnp.stack([solution, coef])
    padded = extended(stacked, (("bx", 3), ("by", 2)), 1)
    padded = jnp.pad(padded, ((0, 0), (1, 1), (0, 0), (0, 0)))
    values = padded[0]
    padcoef = padded[1]
    slices = [
        (slice(2, None), slice(1, -1), slice(1, -1)),
        (slice(0, -2), slice(1, -1), slice(1, -1)),
        (slice(1, -1), slice(2, None), slice(1, -1)),
        (slice(1, -1), slice(0, -2), slice(1, -1)),
        (slice(1, -1), slice(1, -1), slice(2, None)),
        (slice(1, -1), slice(1, -1), slice(0, -2)),
    ]
    result = jnp.zeros(solution.shape, jnp.float32)
    for where_at in slices:
        neighbour = values[where_at]
        ncoef = padcoef[where_at]
        face = jnp.where(ncoef > 0, 2.0 * coef * ncoef / (coef + ncoef), coef)
        result = result + face * (solution - neighbour)
    return result


def x_high(values, matrix_rows):
    columns = matrix_rows.astype(jnp.float32)
    return jnp.einsum(
        "kjx,mx->kjm",
        lax.all_gather(values, "bx", axis=2, tiled=True),
        columns,
        precision=lax.Precision.HIGHEST,
    )


def y_low(values, matrix_rows):
    return jnp.einsum(
        "kjm,nj->knm",
        lax.all_gather(values, "by", axis=1, tiled=True),
        matrix_rows,
        preferred_element_type=jnp.float32,
    )


def on_device_plain(
    solution,
    source,
    class_ids,
    conductivity,
    spacing_x,
    spacing_y,
    spacing_z,
    forward_x,
    forward_y,
    forward_z,
    inverse_x,
    inverse_y,
    inverse_z,
    eigen_x,
    eigen_y,
    eigen_z,
):
    highest = lax.Precision.HIGHEST
    coef = coefficients(class_ids, conductivity)
    operated = operate(solution, coef)
    weights = spacing_z[:, None, None] * spacing_y[None, :, None] * spacing_x[None, None, :]
    restricted = (weights * (source - operated)).astype(jnp.bfloat16)
    modes_xy = x_high(y_low(restricted, forward_y), forward_x)
    modes = jnp.einsum("qk,knm->qnm", forward_z.astype(jnp.float32), modes_xy, precision=highest)
    divisor = eigen_x[None, None, :] + eigen_y[None, :, None] + eigen_z[:, None, None] + shift_value
    scaled = modes / divisor
    spectral = jnp.einsum(
        "kq,qnm->knm", inverse_z.astype(jnp.float32), scaled, precision=highest
    ).astype(jnp.bfloat16)
    field = x_high(y_low(spectral, inverse_y), inverse_x)
    return solution + weights * field


def tiled(mesh, shape):
    bx, by = mesh.shape["bx"], mesh.shape["by"]
    planes, rows, columns = shape
    rows, columns = rows // by, columns // bx
    if bx % 2 or by % 2 or rows % LANES or columns % (LANES * (by // 2)):
        return False
    return (2 * planes) <= LANES and columns // (by // 2) == LANES and by % bx == 0


def solution(mesh):
    in_specs = (
        P(None, "by", "bx"),
        P(None, "by", "bx"),
        P(None, "by", "bx"),
        P(),
        P("bx"),
        P("by"),
        P(),
        P("bx", None),
        P("by", None),
        P(),
        P("bx", None),
        P("by", None),
        P(),
        P("bx"),
        P("by"),
        P(),
    )
    out_specs = P(None, "by", "bx")

    def whole(*operands):
        body = on_device_tiled if tiled(mesh, operands[0].shape) else on_device_plain
        return jax.shard_map(
            body, mesh=mesh, in_specs=in_specs, out_specs=out_specs, check_vma=False
        )(*operands)

    return whole
```
